32 devices in a mesh: parts: 2 (over y), row: 4 (over z), col: 4 (over x, core).
Axes of the slice: x: 2, y: 2, z: 4, core: 2. Of those that a mesh axis runs over, the one named last changes fastest.
Arguments:
- features: bfloat16 [16384, 256], P(('parts', 'row', 'col')), parts along dimension 0, may hold values from -6 to 6
- weight: bfloat16 [256, 256], replicated, may hold values from -0.375 to 0.375
- bias: float32 [256], replicated, may hold values from -3 to 3
- tiles: bfloat16 [8, 4, 256, 128, 128], P(('parts', 'row'), 'col'), parts along dimension 0, may hold values from -0.0625 to 0.0625
- tile_out: int32 [8, 4, 256], P(('parts', 'row'), 'col'), parts along dimension 0, may hold values from 0 to 15
- tile_in: int32 [8, 4, 256], P(('parts', 'row'), 'col'), parts along dimension 0, may hold values from 0 to 15
- tile_count: int32 [8, 4], P(('parts', 'row'), 'col'), parts along dimension 0, may hold values from 64 to 256, as said below
- cotangent: bfloat16 [16384, 256], P(('parts', 'row', 'col')), parts along dimension 0, may hold values from -6 to 6
Outputs:
- output: bfloat16 [16384, 256], P(('parts', 'row', 'col')), parts along dimension 0
- grad_features: bfloat16 [16384, 256], P(('parts', 'row', 'col')), parts along dimension 0
- grad_weight: float32 [512, 256], P('parts'), parts along dimension 0
- grad_bias: float32 [512], P('parts'), parts along dimension 0
The draws below stay inside these ranges and needn't reach their ends.
There are 2 independent parts, one for each index of `parts`. The reference program is written for one: setup_inputs(seed, part) draws one part's arguments, and reference() takes and returns one part's arrays. A program takes and returns all parts, laid end to end along the dimension named above; an argument that names none is the same for every part. Nothing has to cross between parts.
Inputs may be any that keep to these rules, and one draw needn't show every extreme that they name: The live slots of a cell are its first tile_count slots; at least one cell has all 256 slots live.
All inputs are finite; a program needn't handle non-finite values.
Results may differ from the reference program's by a relative error of at most 0.006.
Values may be sent and summed in bfloat16 or wider, within the bound.
A program may use at most 128 MiB of HBM per device.

```python
import math
import jax
import jax.numpy as jnp
from jax import lax

D = 256
BLOCK = 128
CL_DEV = 4
TILES_CELL = 256
OUT_CL = 16
IN_CL = 16
CLUSTERS = 64
NODES = 8192
N_ROW = 4
N_COL = 4


def draw_tile_count(key, part):
    key = jax.random.fold_in(key, 11)
    first_key, second_key = jax.random.split(key)
    divisor = jax.random.randint(first_key, (N_ROW * N_COL,), 1, 5)
    counts = TILES_CELL // divisor
    chosen = jax.random.randint(second_key, (), 0, N_ROW * N_COL)
    counts = jnp.where(jnp.arange(N_ROW * N_COL) == chosen, TILES_CELL, counts)
    return counts.reshape(N_ROW, N_COL).astype(jnp.int32)


def place_ends(values, key, low, high):
    shape = values.shape
    index_at = [jax.random.randint(jax.random.fold_in(key, axis), (), 0, shape[axis]) for axis in range(len(shape))]
    values = values.at[tuple(index_at)].set(low)
    longest = shape.index(max(shape))
    index_at[longest] = (index_at[longest] + 1) % shape[longest]
    return values.at[tuple(index_at)].set(high)


def levels(key, shape, cuts, smallest, top_value):
    def one(axis_at, shards_of):
        steps = jax.random.uniform(jax.random.fold_in(jax.random.fold_in(key, 6), axis_at), (shards_of,), jnp.float32, smallest / len(cuts), top_value / len(cuts))
        return jnp.repeat(jnp.exp(steps), shape[axis_at] // shards_of).reshape((-1,) + (1,) * (len(shape) - axis_at - 1))

    factor_of = one(*cuts[0])
    for cut in cuts[1:]:
        factor_of = factor_of * one(*cut)
    return factor_of


def noise(own_key, shape, deviation, reach, cuts=(), held_as=jnp.bfloat16):
    loudness = levels(own_key, shape, cuts, -0.22, 0.18) if cuts else 1.0
    result = jax.random.normal(own_key, shape, jnp.float32) * deviation * loudness
    return jnp.minimum(jnp.maximum(result, -reach), reach).astype(held_as)


def setup_inputs(seed: int = 0, part: int = 0) -> dict:
    keys = jax.random.split(jax.random.key(seed), 9)
    own_keys = jax.random.split(jax.random.fold_in(keys[8], part), 9)
    features = noise(own_keys[0], (NODES, D), 1.0, 6.0, ((0, 16),))
    weight = noise(keys[1], (D, D), D ** -0.5, 0.375)
    bias = noise(keys[2], (D,), 0.5, 3.0, (), jnp.float32)
    tiles = noise(own_keys[3], (N_ROW, N_COL, TILES_CELL, BLOCK, BLOCK), (TILES_CELL * BLOCK // CL_DEV) ** -0.5, 0.0625, ((0, 4), (1, 4)))
    tile_out = place_ends(jax.random.randint(own_keys[4], (N_ROW, N_COL, TILES_CELL), 0, OUT_CL), jax.random.fold_in(own_keys[4], 1), 0, OUT_CL - 1).astype(jnp.int32)
    tile_in = place_ends(jax.random.randint(own_keys[5], (N_ROW, N_COL, TILES_CELL), 0, IN_CL), jax.random.fold_in(own_keys[5], 1), 0, IN_CL - 1).astype(jnp.int32)
    tile_count = draw_tile_count(jax.random.fold_in(jax.random.fold_in(keys[8], part), 71), part)
    cotangent = noise(own_keys[7], (NODES, D), 1.0, 6.0, ((0, 16),))
    return {"features": features, "weight": weight, "bias": bias, "tiles": tiles, "tile_out": tile_out, "tile_in": tile_in, "tile_count": tile_count, "cotangent": cotangent}


def cluster_ids(cell_id, out_local, in_local):
    row_id = cell_id // N_COL
    col_id = cell_id % N_COL
    out_glob = (out_local // CL_DEV * N_COL + col_id) * CL_DEV + out_local % CL_DEV
    in_glob = row_id * IN_CL + in_local
    return (out_glob.astype(jnp.int32), in_glob.astype(jnp.int32))

def reference(features, weight, bias, tiles, tile_out, tile_in, tile_count, cotangent):
    cell_total = N_ROW * N_COL
    projected = jnp.dot(features, weight, preferred_element_type=jnp.float32).astype(jnp.bfloat16)
    source = projected.reshape(CLUSTERS, BLOCK, D)
    flat_tiles = tiles.reshape(cell_total, TILES_CELL, BLOCK, BLOCK)
    flat_out = tile_out.reshape(cell_total, TILES_CELL)
    flat_in = tile_in.reshape(cell_total, TILES_CELL)
    flat_count = tile_count.reshape(cell_total)
    cell_list = jnp.arange(cell_total, dtype=jnp.int32)
    slot_ids = jnp.arange(TILES_CELL, dtype=jnp.int32)

    def forward_cell(running, inputs):
        cell_id, cell_tiles, out_local, in_local, live_count = inputs
        out_glob, in_glob = cluster_ids(cell_id, out_local, in_local)
        is_live = (slot_ids < live_count).astype(jnp.float32)
        picked = source[in_glob].astype(jnp.float32)
        products = jnp.einsum('tij,tjd->tid', cell_tiles.astype(jnp.float32), picked)
        products = products * is_live[:, None, None]
        return (running.at[out_glob].add(products), None)
    initial = jnp.zeros((CLUSTERS, BLOCK, D), jnp.float32)
    summed, _ = lax.scan(forward_cell, initial, (cell_list, flat_tiles, flat_out, flat_in, flat_count))
    hidden = summed.reshape(NODES, D) + bias
    output = jax.nn.silu(hidden).astype(jnp.bfloat16)
    gate_value = jax.nn.sigmoid(hidden)
    grad_hidden = (cotangent.astype(jnp.float32) * gate_value * (1.0 + hidden * (1.0 - gate_value))).astype(jnp.bfloat16)
    targets = grad_hidden.reshape(CLUSTERS, BLOCK, D)

    def backward_cell(running, inputs):
        cell_id, cell_tiles, out_local, in_local, live_count = inputs
        out_glob, in_glob = cluster_ids(cell_id, out_local, in_local)
        is_live = (slot_ids < live_count).astype(jnp.float32)
        picked = targets[out_glob].astype(jnp.float32)
        products = jnp.einsum('tji,tjd->tid', cell_tiles.astype(jnp.float32), picked)
        products = products * is_live[:, None, None]
        return (running.at[in_glob].add(products), None)
    grad_summed, _ = lax.scan(backward_cell, initial, (cell_list, flat_tiles, flat_out, flat_in, flat_count))
    grad_proj = grad_summed.reshape(NODES, D).astype(jnp.bfloat16)
    grad_features = jnp.dot(grad_proj, weight.T, preferred_element_type=jnp.float32).astype(jnp.bfloat16)
    factor = 1.0 / math.sqrt(NODES)
    grad_weight = jnp.dot(features.T, grad_proj, preferred_element_type=jnp.float32) * factor
    grad_bias = lax.optimization_barrier(jnp.sum(grad_hidden.astype(jnp.float32), axis=0)) * factor
    return (output, grad_features, grad_weight, grad_bias)
```

```python
import functools
import math

import jax
import jax.numpy as jnp
from jax import lax
from jax.experimental import pallas as pl
from jax.experimental.pallas import tpu as pltpu
from jax.sharding import PartitionSpec as P

MESH = pl.DeviceIdType.MESH


def accumulate(cell_tiles, from_ids, into_ids, live_count, source, into_count, pattern):
    slot_count = cell_tiles.shape[0]
    from_count = source.shape[0]
    cluster_size = source.shape[1]
    feat_width = source.shape[2]
    span_size = 32
    flat_source = source.reshape(from_count, cluster_size * feat_width)
    initial = jnp.zeros((into_count, cluster_size * feat_width), jnp.float32)
    from_range = jnp.arange(from_count, dtype=jnp.int32)
    into_range = jnp.arange(into_count, dtype=jnp.int32)

    def one_block(block_index, running):
        offset = block_index * span_size
        some_tiles = lax.dynamic_slice_in_dim(cell_tiles, offset, span_size, 0)
        from_block = lax.dynamic_slice_in_dim(from_ids, offset, span_size, 0)
        into_block = lax.dynamic_slice_in_dim(into_ids, offset, span_size, 0)
        is_live = offset + jnp.arange(span_size, dtype=jnp.int32) < live_count
        select = (from_block[:, None] == from_range[None, :]).astype(jnp.bfloat16)
        picked = jnp.dot(select, flat_source, preferred_element_type=jnp.float32).astype(
            jnp.bfloat16
        )
        picked = picked.reshape(span_size, cluster_size, feat_width)
        products = jnp.einsum(pattern, some_tiles, picked, preferred_element_type=jnp.float32)
        placing = ((into_range[:, None] == into_block[None, :]) & is_live[None, :]).astype(
            jnp.float32
        )
        added = jnp.dot(
            placing,
            products.reshape(span_size, cluster_size * feat_width),
            precision=lax.Precision.HIGHEST,
            preferred_element_type=jnp.float32,
        )
        return running + added

    block_total = (live_count + span_size - 1) // span_size
    result = lax.fori_loop(0, block_total, one_block, initial)
    return result.reshape(into_count, cluster_size, feat_width)


def slope(hidden, cotangent):
    gate_value = jax.nn.sigmoid(hidden)
    return (
        cotangent.astype(jnp.float32) * gate_value * (1.0 + hidden * (1.0 - gate_value))
    ).astype(jnp.bfloat16)


def body(features, weight, bias, tiles, tile_out, tile_in, tile_count, cotangent):
    slot_count = tiles.shape[2]
    cluster_size = tiles.shape[3]
    feat_width = features.shape[1]
    own_rows = features.shape[0]
    own_clusters = own_rows // cluster_size
    cell_tiles = tiles.reshape(slot_count, cluster_size, cluster_size)
    out_local = tile_out.reshape(slot_count)
    in_local = tile_in.reshape(slot_count)
    live_count = tile_count.reshape(())
    row_devices = lax.axis_size("row")
    col_devices = lax.axis_size("col")
    into_clusters = own_clusters * row_devices
    from_clusters = own_clusters * col_devices
    projected = jnp.dot(features, weight, preferred_element_type=jnp.float32).astype(jnp.bfloat16)
    inputs = lax.all_gather(projected, "col", axis=0, tiled=True)
    partials = accumulate(
        cell_tiles,
        in_local,
        out_local,
        live_count,
        inputs.reshape(from_clusters, cluster_size, feat_width),
        into_clusters,
        "tij,tjd->tid",
    )
    partials = partials.reshape(into_clusters * cluster_size, feat_width)
    summed = lax.psum_scatter(partials, "row", scatter_dimension=0, tiled=True)
    hidden = summed + bias
    output = jax.nn.silu(hidden).astype(jnp.bfloat16)
    own_grad = slope(hidden, cotangent)
    targets = lax.all_gather(own_grad, "row", axis=0, tiled=True)
    grad_partials = accumulate(
        cell_tiles,
        out_local,
        in_local,
        live_count,
        targets.reshape(into_clusters, cluster_size, feat_width),
        from_clusters,
        "tji,tjd->tid",
    )
    grad_partials = grad_partials.reshape(from_clusters * cluster_size, feat_width)
    grad_proj = lax.psum_scatter(grad_partials, "col", scatter_dimension=0, tiled=True).astype(
        jnp.bfloat16
    )
    grad_features = jnp.dot(grad_proj, weight.T, preferred_element_type=jnp.float32).astype(
        jnp.bfloat16
    )
    local_weight = jnp.dot(features.T, grad_proj, preferred_element_type=jnp.float32)
    local_bias = jnp.sum(own_grad.astype(jnp.float32), axis=0)
    grad_weight, grad_bias = lax.psum((local_weight, local_bias), ("row", "col"))
    factor = 1.0 / math.sqrt(own_rows * row_devices * col_devices)
    return (output, grad_features, grad_weight * factor, grad_bias * factor)

def build_kernel(count_ref, out_ids, in_ids, tiles_ref, dense_ref, sums):
    step = pl.program_id(0)
    slots, size = tiles_ref.shape[0], tiles_ref.shape[1]
    side = dense_ref.shape[0] // size
    wide = dense_ref.shape[1] // size
    spare = side * wide

    @pl.when(step == 0)
    def _():
        sums[...] = jnp.zeros_like(sums)

    def add(slot, _):
        where = step * slots + slot
        pair = out_ids[where] * wide + in_ids[where]
        pair = jnp.where(where < count_ref[0], pair, spare)
        sums[pair] += tiles_ref[slot].astype(jnp.float32)
        return 0

    lax.fori_loop(0, slots, add, 0, unroll=8)

    @pl.when(step == pl.num_programs(0) - 1)
    def _():
        def write(o, _):
            rows = pl.ds(pl.multiple_of(o * size, size), size)
            for i in range(wide):
                dense_ref[rows, pl.ds(i * size, size)] = sums[o * wide + i].astype(jnp.bfloat16)
            return 0

        lax.fori_loop(0, side, write, 0)


def build_dense(cell_tiles, out_local, in_local, live_count, side, wide):
    slot_count, size, _ = cell_tiles.shape
    span = 32
    return pl.pallas_call(
        build_kernel,
        out_shape=jax.ShapeDtypeStruct((side * size, wide * size), jnp.bfloat16),
        grid_spec=pltpu.PrefetchScalarGridSpec(
            num_scalar_prefetch=3,
            grid=(slot_count // span,),
            in_specs=[pl.BlockSpec((span, size, size), lambda s, *_: (s, 0, 0))],
            out_specs=pl.BlockSpec((side * size, wide * size), lambda s, *_: (0, 0)),
            scratch_shapes=[pltpu.VMEM((side * wide + 1, size, size), jnp.float32)],
        ),
        compiler_params=pltpu.CompilerParams(vmem_limit_bytes=48 * 2**20),
        cost_estimate=pl.CostEstimate(
            flops=slot_count * size * size * 40, bytes_accessed=4 * slot_count * size * size, transcendentals=0
        ),
        name="dense_cell",
    )(live_count, out_local, in_local, cell_tiles)


def layer_kernel(
    R, C, S, factor,
    a_ref, p_ref, feat_ref, w_ref, bias_ref, cot_ref,
    out_ref, gfeat_ref, gw_ref, gb_ref,
    part_send, part_recv, own, grads, gsum, back_send, back_recv, back_own,
    w_send, w_recv, wr_recv, wc_recv,
    s1, r1, s2, r2, s3, r3, s4, r4, s5, r5, s6, r6,
):
    my_row = lax.axis_index("row")
    my_col = lax.axis_index("col")
    n, d = feat_ref.shape
    hb = n // S
    f32, bf16 = jnp.float32, jnp.bfloat16
    barrier = pltpu.get_barrier_semaphore()

    def row_of(m):
        return lax.rem(my_row + m, R)

    def col_of(m):
        return lax.rem(my_col + m, C)

    for m in range(1, R):
        pl.semaphore_signal(barrier, inc=1, device_id={"row": row_of(m)}, device_id_type=MESH)
    for m in range(1, C):
        pl.semaphore_signal(barrier, inc=1, device_id={"col": col_of(m)}, device_id_type=MESH)

    def remote(src, dst, send, recv, where):
        return pltpu.make_async_remote_copy(
            src_ref=src, dst_ref=dst, send_sem=send, recv_sem=recv, device_id=where, device_id_type=MESH
        )

    sent = []
    order = [2, 1, 3] if R == 4 else list(range(1, R))
    corder = [2, 3, 1] if C == 4 else list(range(1, C))
    first = [None] * (R * S)
    waited = False
    for h in range(S):
        for m in order + [0]:
            start = pl.multiple_of(row_of(m) * n + h * hb, hb)
            total = jnp.dot(a_ref[pl.ds(start, hb), :], p_ref[...], preferred_element_type=f32)
            if m == 0:
                own[h] = total
                continue
            part_send[m - 1, h] = total.astype(bf16)
            if not waited:
                pl.semaphore_wait(barrier, R + C - 2)
                waited = True
            copy = remote(
                part_send.at[m - 1, h], part_recv.at[m - 1, h],
                s1.at[m - 1, h], r1.at[m - 1, h], {"row": row_of(m)},
            )
            copy.start()
            sent.append(copy)
            first[m * S + h] = copy

    gbias = jnp.zeros((1, d), f32)
    second = {}
    for h in range(S):
        rows = pl.ds(h * hb, hb)
        hidden = own[h] + bias_ref[...]
        for m in [1, 3, 2] if R == 4 else range(1, R):
            first[m * S + h].wait_recv()
            hidden = hidden + part_recv[m - 1, h].astype(f32)
        gate = jax.nn.sigmoid(hidden)
        g = cot_ref[rows, :].astype(f32) * gate * (1.0 + hidden * (1.0 - gate))
        g = g.astype(bf16).astype(f32)
        grads[0, h] = g.T.astype(bf16)
        for m in order:
            copy = remote(
                grads.at[0, h], grads.at[m, h], s2.at[m - 1, h], r2.at[m - 1, h], {"row": row_of(m)}
            )
            copy.start()
            sent.append(copy)
            second[m, h] = copy
        out_ref[rows, :] = (hidden * gate).astype(bf16)
        gbias = gbias + jnp.sum(g, axis=0, keepdims=True)

    steps = [(0, h) for h in range(S)]
    steps += [(m, h) for h in range(S) for m in ([1, 3, 2] if R == 4 else range(1, R))]
    third = {}
    for at, (m, h) in enumerate(steps):
        if m:
            second[m, h].wait_recv()
        start = pl.multiple_of(lax.rem(my_row + R - m, R) * n + h * hb, hb)
        for k in corder + [0]:
            c0 = pl.multiple_of(col_of(k) * n, n)
            new = jnp.dot(
                grads[m, h], a_ref[pl.ds(start, hb), pl.ds(c0, n)], preferred_element_type=f32
            )
            if at:
                new = gsum[k] + new
            if at < len(steps) - 1:
                gsum[k] = new
            elif k == 0:
                gsum[0] = new
            else:
                back_send[k - 1] = new.astype(bf16)
                copy = remote(
                    back_send.at[k - 1], back_recv.at[k - 1], s3.at[k - 1], r3.at[k - 1], {"col": col_of(k)}
                )
                copy.start()
                sent.append(copy)
                third[k] = copy

    total = gsum[0]
    for k in [1, 2, 3] if C == 4 else range(1, C):
        third[k].wait_recv()
        total = total + back_recv[k - 1].astype(f32)
    gproj = total.astype(bf16)
    gweight = jnp.dot(gproj, feat_ref[...], preferred_element_type=f32).T * factor
    gbias = gbias * factor
    q = d // C
    for k in range(C):
        w_send[k, 0:q] = gweight[k * q : (k + 1) * q].astype(bf16)
        w_send[k, q : q + 16] = jnp.broadcast_to(gbias, (16, d)).astype(bf16)
    fourth = []
    for k in corder:
        copy = remote(
            w_send.at[col_of(k)], w_recv.at[my_col], s4.at[k - 1], r4.at[k - 1], {"col": col_of(k)}
        )
        copy.start()
        fourth.append(copy)
    w_recv[my_col] = w_send[my_col]
    back_own[...] = jnp.dot(w_ref[...], gproj, preferred_element_type=f32)
    gfeat_ref[...] = back_own[...].T.astype(bf16)
    for copy in fourth:
        copy.wait_recv()
    part = w_recv[0].astype(f32)
    for k in range(1, C):
        part = part + w_recv[k].astype(f32)
    wr_recv[my_row] = part.astype(bf16)
    fifth = []
    for m in order:
        copy = remote(
            wr_recv.at[my_row], wr_recv.at[my_row], s5.at[m - 1], r5.at[m - 1], {"row": row_of(m)}
        )
        copy.start()
        fifth.append(copy)
    for copy in fifth:
        copy.wait_recv()
    part = wr_recv[0].astype(f32)
    for m in range(1, R):
        part = part + wr_recv[m].astype(f32)
    gb_ref[...] = part[q : q + 1]
    wc_recv[my_col] = part[0:q].astype(bf16)
    sixth = []
    for k in corder:
        copy = remote(
            wc_recv.at[my_col], wc_recv.at[my_col], s6.at[k - 1], r6.at[k - 1], {"col": col_of(k)}
        )
        copy.start()
        sixth.append(copy)
    for copy in sixth:
        copy.wait_recv()
    for k in range(C):
        gw_ref[pl.ds(k * q, q), :] = wc_recv[k].astype(f32)
    for copy in sent + fourth + fifth + sixth:
        copy.wait_send()


def dense_body(features, weight, bias, tiles, tile_out, tile_in, tile_count, cotangent):
    slots, size = tiles.shape[2], tiles.shape[3]
    n, d = features.shape
    R, C = lax.axis_size("row"), lax.axis_size("col")
    own = n // size
    side, wide = own * R, own * C
    projected = jnp.dot(features, weight, preferred_element_type=jnp.float32).astype(jnp.bfloat16)
    dense = build_dense(
        tiles.reshape(slots, size, size), tile_out.reshape(slots), tile_in.reshape(slots),
        tile_count.reshape(1), side, wide,
    )
    me = lax.axis_index("col")
    inputs = jnp.zeros((wide * size, d), jnp.bfloat16)
    inputs = lax.dynamic_update_slice(inputs, projected, (me * n, 0))
    for m in range(1, C):
        got = lax.ppermute(projected, "col", [(c, (c + m) % C) for c in range(C)])
        inputs = lax.dynamic_update_slice(inputs, got, ((me + C - m) % C * n, 0))
    S = 2
    hb = n // S
    q = d // C
    bf16, f32 = jnp.bfloat16, jnp.float32
    vm = pl.BlockSpec(memory_space=pltpu.VMEM)
    dma = pltpu.SemaphoreType.DMA
    output, gfeat, gw, gb = pl.pallas_call(
        functools.partial(layer_kernel, R, C, S, 1.0 / math.sqrt(n * R * C)),
        out_shape=(
            jax.ShapeDtypeStruct((n, d), bf16),
            jax.ShapeDtypeStruct((n, d), bf16),
            jax.ShapeDtypeStruct((d, d), f32),
            jax.ShapeDtypeStruct((1, d), f32),
        ),
        in_specs=[vm] * 6,
        out_specs=(vm,) * 4,
        scratch_shapes=[
            pltpu.VMEM((R - 1, S, hb, d), bf16),
            pltpu.VMEM((R - 1, S, hb, d), bf16),
            pltpu.VMEM((S, hb, d), f32),
            pltpu.VMEM((R, S, d, hb), bf16),
            pltpu.VMEM((C, d, n), f32),
            pltpu.VMEM((C - 1, d, n), bf16),
            pltpu.VMEM((C - 1, d, n), bf16),
            pltpu.VMEM((d, n), f32),
            pltpu.VMEM((C, q + 16, d), bf16),
            pltpu.VMEM((C, q + 16, d), bf16),
            pltpu.VMEM((R, q + 16, d), bf16),
            pltpu.VMEM((C, q, d), bf16),
            dma((R - 1, S)), dma((R - 1, S)), dma((R - 1, S)), dma((R - 1, S)),
            dma((C - 1,)), dma((C - 1,)), dma((C - 1,)), dma((C - 1,)),
            dma((R - 1,)), dma((R - 1,)), dma((C - 1,)), dma((C - 1,)),
        ],
        compiler_params=pltpu.CompilerParams(
            collective_id=0, has_side_effects=True, vmem_limit_bytes=40 * 2**20
        ),
        cost_estimate=pl.CostEstimate(
            flops=4 * n * R * n * C * d, bytes_accessed=2 * n * R * n * C, transcendentals=n * d
        ),
        name="layer",
    )(dense, inputs, features, weight, bias.reshape(1, d), cotangent)
    return output, gfeat, gw, gb.reshape(d)


def layer_body(features, *rest):
    cells = lax.axis_size("row") * lax.axis_size("col")
    small = features.shape[0] * features.shape[0] * cells <= 2**22
    return (dense_body if small else body)(features, *rest)


def solution(mesh):
    placed = (
        P(("parts", "row", "col"), None),
        P(),
        P(),
        P(("parts", "row"), "col", None, None, None),
        P(("parts", "row"), "col", None),
        P(("parts", "row"), "col", None),
        P(("parts", "row"), "col"),
        P(("parts", "row", "col"), None),
    )
    return jax.shard_map(
        layer_body,
        mesh=mesh,
        in_specs=placed,
        out_specs=(
            P(("parts", "row", "col"), None),
            P(("parts", "row", "col"), None),
            P("parts", None),
            P("parts"),
        ),
        check_vma=False,
    )
```

```python
import functools
import math

import jax
import jax.numpy as jnp
from jax import lax
from jax.experimental import pallas as pl
from jax.experimental.pallas import tpu as pltpu
from jax.sharding import PartitionSpec as P

MESH = pl.DeviceIdType.MESH


def accumulate(cell_tiles, from_ids, into_ids, live_count, source, into_count, pattern):
    slot_count = cell_tiles.shape[0]
    from_count = source.shape[0]
    cluster_size = source.shape[1]
    feat_width = source.shape[2]
    span_size = 32
    flat_source = source.reshape(from_count, cluster_size * feat_width)
    initial = jnp.zeros((into_count, cluster_size * feat_width), jnp.float32)
    from_range = jnp.arange(from_count, dtype=jnp.int32)
    into_range = jnp.arange(into_count, dtype=jnp.int32)

    def one_block(block_index, running):
        offset = block_index * span_size
        some_tiles = lax.dynamic_slice_in_dim(cell_tiles, offset, span_size, 0)
        from_block = lax.dynamic_slice_in_dim(from_ids, offset, span_size, 0)
        into_block = lax.dynamic_slice_in_dim(into_ids, offset, span_size, 0)
        is_live = offset + jnp.arange(span_size, dtype=jnp.int32) < live_count
        select = (from_block[:, None] == from_range[None, :]).astype(jnp.bfloat16)
        picked = jnp.dot(select, flat_source, preferred_element_type=jnp.float32).astype(
            jnp.bfloat16
        )
        picked = picked.reshape(span_size, cluster_size, feat_width)
        products = jnp.einsum(pattern, some_tiles, picked, preferred_element_type=jnp.float32)
        placing = ((into_range[:, None] == into_block[None, :]) & is_live[None, :]).astype(
            jnp.float32
        )
        added = jnp.dot(
            placing,
            products.reshape(span_size, cluster_size * feat_width),
            precision=lax.Precision.HIGHEST,
            preferred_element_type=jnp.float32,
        )
        return running + added

    block_total = (live_count + span_size - 1) // span_size
    result = lax.fori_loop(0, block_total, one_block, initial)
    return result.reshape(into_count, cluster_size, feat_width)


def slope(hidden, cotangent):
    gate_value = jax.nn.sigmoid(hidden)
    return (
        cotangent.astype(jnp.float32) * gate_value * (1.0 + hidden * (1.0 - gate_value))
    ).astype(jnp.bfloat16)


def body(features, weight, bias, tiles, tile_out, tile_in, tile_count, cotangent):
    slot_count = tiles.shape[2]
    cluster_size = tiles.shape[3]
    feat_width = features.shape[1]
    own_rows = features.shape[0]
    own_clusters = own_rows // cluster_size
    cell_tiles = tiles.reshape(slot_count, cluster_size, cluster_size)
    out_local = tile_out.reshape(slot_count)
    in_local = tile_in.reshape(slot_count)
    live_count = tile_count.reshape(())
    row_devices = lax.axis_size("row")
    col_devices = lax.axis_size("col")
    into_clusters = own_clusters * row_devices
    from_clusters = own_clusters * col_devices
    projected = jnp.dot(features, weight, preferred_element_type=jnp.float32).astype(jnp.bfloat16)
    inputs = lax.all_gather(projected, "col", axis=0, tiled=True)
    partials = accumulate(
        cell_tiles,
        in_local,
        out_local,
        live_count,
        inputs.reshape(from_clusters, cluster_size, feat_width),
        into_clusters,
        "tij,tjd->tid",
    )
    partials = partials.reshape(into_clusters * cluster_size, feat_width)
    summed = lax.psum_scatter(partials, "row", scatter_dimension=0, tiled=True)
    hidden = summed + bias
    output = jax.nn.silu(hidden).astype(jnp.bfloat16)
    own_grad = slope(hidden, cotangent)
    targets = lax.all_gather(own_grad, "row", axis=0, tiled=True)
    grad_partials = accumulate(
        cell_tiles,
        out_local,
        in_local,
        live_count,
        targets.reshape(into_clusters, cluster_size, feat_width),
        from_clusters,
        "tji,tjd->tid",
    )
    grad_partials = grad_partials.reshape(from_clusters * cluster_size, feat_width)
    grad_proj = lax.psum_scatter(grad_partials, "col", scatter_dimension=0, tiled=True).astype(
        jnp.bfloat16
    )
    grad_features = jnp.dot(grad_proj, weight.T, preferred_element_type=jnp.float32).astype(
        jnp.bfloat16
    )
    local_weight = jnp.dot(features.T, grad_proj, preferred_element_type=jnp.float32)
    local_bias = jnp.sum(own_grad.astype(jnp.float32), axis=0)
    grad_weight, grad_bias = lax.psum((local_weight, local_bias), ("row", "col"))
    factor = 1.0 / math.sqrt(own_rows * row_devices * col_devices)
    return (output, grad_features, grad_weight * factor, grad_bias * factor)

def build_kernel(count_ref, out_ids, in_ids, tiles_hbm, dense_hbm, sums, held, dense, in_sem, out_sem):
    slots, size = held.shape[0], held.shape[1]
    side = dense.shape[0] // size
    wide = dense.shape[1] // size
    spare = side * wide
    spans = in_sem.shape[0]
    span = slots // spans

    def fetch(step):
        part = pl.ds(step * span, span)
        return pltpu.make_async_copy(tiles_hbm.at[part], held.at[part], in_sem.at[step])

    for step in range(spans):
        fetch(step).start()

    def clear(at, _):
        sums[at] = jnp.zeros_like(sums[0])
        return 0

    lax.fori_loop(0, spare, clear, 0, unroll=8)

    def add(where, _):
        pair = out_ids[where] * wide + in_ids[where]
        pair = jnp.where(where < count_ref[0], pair, spare)
        sums[pair] += held[where].astype(jnp.float32)
        return 0

    for step in range(spans):
        fetch(step).wait()
        lax.fori_loop(step * span, (step + 1) * span, add, 0, unroll=8)

    def put(o):
        rows = pl.ds(pl.multiple_of(o * size, size), size)
        return pltpu.make_async_copy(dense.at[rows], dense_hbm.at[rows], out_sem.at[o])

    def write(o, _):
        rows = pl.ds(pl.multiple_of(o * size, size), size)
        for i in range(wide):
            dense[rows, pl.ds(i * size, size)] = sums[o * wide + i].astype(jnp.bfloat16)
        put(o).start()
        return 0

    lax.fori_loop(0, side, write, 0)
    for o in range(side):
        put(o).wait()


def build_dense(cell_tiles, out_local, in_local, live_count, side, wide):
    slot_count, size, _ = cell_tiles.shape
    spans = 8
    return pl.pallas_call(
        build_kernel,
        out_shape=jax.ShapeDtypeStruct((side * size, wide * size), jnp.bfloat16),
        grid_spec=pltpu.PrefetchScalarGridSpec(
            num_scalar_prefetch=3,
            grid=(1,),
            in_specs=[pl.BlockSpec(memory_space=pl.ANY)],
            out_specs=pl.BlockSpec(memory_space=pl.ANY),
            scratch_shapes=[
                pltpu.VMEM((side * wide + 1, size, size), jnp.float32),
                pltpu.VMEM((slot_count, size, size), jnp.bfloat16),
                pltpu.VMEM((side * size, wide * size), jnp.bfloat16),
                pltpu.SemaphoreType.DMA((spans,)),
                pltpu.SemaphoreType.DMA((side,)),
            ],
        ),
        compiler_params=pltpu.CompilerParams(vmem_limit_bytes=56 * 2**20),
        cost_estimate=pl.CostEstimate(
            flops=slot_count * size * size * 40, bytes_accessed=4 * slot_count * size * size, transcendentals=0
        ),
        name="dense_cell",
    )(live_count, out_local, in_local, cell_tiles)


def layer_kernel(
    R, C, S, factor,
    a_hbm, p_ref, feat_ref, w_ref, bias_ref, cot_ref,
    out_ref, gfeat_ref, gw_ref, gb_ref,
    a_ref, part, part_send, part_recv, hid, grads, gsum, back_send, back_recv, back_own,
    w_send, w_recv, wr_recv, wc_recv,
    a_sem, s1, r1, s2, s2b, r2, s3, r3, s4, r4, s5, r5, s6, r6,
):
    my_row = lax.axis_index("row")
    my_col = lax.axis_index("col")
    n, d = feat_ref.shape
    hb = n // S
    f32, bf16 = jnp.float32, jnp.bfloat16
    barrier = pltpu.get_barrier_semaphore()

    def row_of(m):
        return lax.rem(my_row + m, R)

    def col_of(m):
        return lax.rem(my_col + m, C)

    for m in range(1, R):
        pl.semaphore_signal(barrier, inc=1, device_id={"row": row_of(m)}, device_id_type=MESH)
    for m in range(1, C):
        pl.semaphore_signal(barrier, inc=1, device_id={"col": col_of(m)}, device_id_type=MESH)

    def remote(src, dst, send, recv, where):
        return pltpu.make_async_remote_copy(
            src_ref=src, dst_ref=dst, send_sem=send, recv_sem=recv, device_id=where, device_id_type=MESH
        )

    order = [2, 1, 3]
    corder = [2, 3, 1]

    high = my_row // 2
    place = (1 - high) * my_row + high * (R - 1 - my_row)

    def at(p):
        return (1 - high) * p + high * (R - 1 - p)

    pair_row = at(1 - place)
    next_row = at(place + 1)
    inner_row = at(2)
    outer, inner = place == 0, place == 1

    targets = [at(3), at(2), pair_row, my_row]
    fetches = []
    for k in range(R):
        rows = pl.ds(pl.multiple_of(targets[k] * n, n), n)
        fetches.append(pltpu.make_async_copy(a_hbm.at[rows], a_ref.at[rows], a_sem.at[k]))
        fetches[k].start()

    def sum_to_pair(k, h):
        return remote(
            part_send.at[k, h], part_recv.at[k, h], s1.at[k, h], r1.at[k, h], {"row": pair_row}
        )

    def sum_to_inner(k, h):
        return remote(
            part_send.at[k, h], part_recv.at[k + 3, h], s1.at[k, h], r1.at[k + 3, h], {"row": inner_row}
        )

    pl.semaphore_wait(barrier, R + C - 2)
    for h in range(S):
        for k in range(R):
            if h == 0:
                fetches[k].wait()
            start = pl.multiple_of(targets[k] * n + h * hb, hb)
            part[k, h] = jnp.dot(a_ref[pl.ds(start, hb), :], p_ref[...], preferred_element_type=f32)
            if k < 3:

                @pl.when(outer)
                def _():
                    part_send[k, h] = part[k, h].astype(bf16)
                    sum_to_pair(k, h).start()

    def grad_to_pair(p, h, sem):
        row = at(p)
        return remote(grads.at[row, h], grads.at[row, h], sem, r2.at[row, h], {"row": pair_row})

    def grad_to_inner(p, h, sem):
        row = at(p)
        return remote(grads.at[row, h], grads.at[row, h], sem, r2.at[row, h], {"row": inner_row})

    gbias = jnp.zeros((1, d), f32)
    own_cols = [3, 2, 1, 0]

    def col_block(k):
        chip, core = my_col // 2, lax.rem(my_col, 2)
        chip = 1 - chip if k >= 2 else chip
        core = 1 - core if k % 2 else core
        return chip * 2 + core

    def back(p, h, first, last):
        row = at(p)
        start = pl.multiple_of(row * n + h * hb, hb)
        for k in own_cols:
            c0 = pl.multiple_of(col_block(k) * n, n)
            new = jnp.dot(
                grads[row, h], a_ref[pl.ds(start, hb), pl.ds(c0, n)], preferred_element_type=f32
            )
            if not first:
                new = gsum[k] + new
            gsum[k] = new
            if last and k in (3, 1):
                back_send[k] = new.astype(bf16)
                back_copy(k).start()

    def back_copy(k):
        if k == 2:
            return remote(back_send.at[2], back_recv.at[2], s3.at[2], r3.at[2], {"col": col_block(2)})
        return remote(back_send.at[k], back_recv.at[k], s3.at[k], r3.at[k], {"col": col_block(1)})

    for h in range(S + 1):
        if h < S:

            @pl.when(inner)
            def _():
                for k in range(3):
                    if k < 2:
                        sum_to_pair(k, h).wait_recv()
                        got = part_recv[k, h]
                    else:
                        sum_to_inner(0, h).wait_recv()
                        got = part_recv[3, h]
                    part_send[k, h] = (part[k, h] + got.astype(f32)).astype(bf16)
                    if k < 2:
                        sum_to_inner(k, h).start()
                    else:
                        sum_to_pair(k, h).start()

            rows = pl.ds(h * hb, hb)
            sum_to_pair(2, h).wait_recv()
            hid[...] = part[3, h] + bias_ref[...] + part_recv[2, h].astype(f32)

            @pl.when(inner)
            def _():
                sum_to_inner(1, h).wait_recv()
                hid[...] += part_recv[4, h].astype(f32)

            hidden = hid[...]
            gate = jax.nn.sigmoid(hidden)
            g = cot_ref[rows, :].astype(f32) * gate * (1.0 + hidden * (1.0 - gate))
            g = g.astype(bf16).astype(f32)
            grads[my_row, h] = g.T.astype(bf16)
            grad_to_pair(place, h, s2.at[0, h]).start()

            @pl.when(inner)
            def _():
                grad_to_inner(place, h, s2b.at[0, h]).start()

            out_ref[rows, :] = (hidden * gate).astype(bf16)
            gbias = gbias + jnp.sum(g, axis=0, keepdims=True)
        if h > 0:
            e = h - 1
            back(place, e, e == 0, False)
            for j, p in enumerate([1 - place, 2, 3]):
                grad_to_pair(p, e, s2.at[0, e]).wait_recv()

                @pl.when(inner)
                def _():
                    if j == 0:
                        grad_to_inner(p, e, s2b.at[1, e]).start()
                    else:
                        grad_to_pair(p, e, s2.at[j, e]).start()

                back(p, e, False, e == S - 1 and j == 2)

    back_copy(3).wait_recv()
    back_send[2] = (gsum[2] + back_recv[3].astype(f32)).astype(bf16)
    back_copy(2).start()
    back_copy(1).wait_recv()
    total = gsum[0] + back_recv[1].astype(f32)
    back_copy(2).wait_recv()
    total = total + back_recv[2].astype(f32)
    gproj = total.astype(bf16)
    gweight = jnp.dot(gproj, feat_ref[...], preferred_element_type=f32).T * factor
    gbias = gbias * factor
    q = d // C
    for k in range(C):
        w_send[k, 0:q] = gweight[k * q : (k + 1) * q].astype(bf16)
        w_send[k, q : q + 16] = jnp.broadcast_to(gbias, (16, d)).astype(bf16)
    fourth = []
    for k in corder:
        copy = remote(
            w_send.at[col_of(k)], w_recv.at[my_col], s4.at[k - 1], r4.at[k - 1], {"col": col_of(k)}
        )
        copy.start()
        fourth.append(copy)
    w_recv[my_col] = w_send[my_col]
    back_own[...] = jnp.dot(w_ref[...], gproj, preferred_element_type=f32)
    gfeat_ref[...] = back_own[...].T.astype(bf16)
    for copy in fourth:
        copy.wait_recv()
    both = w_recv[0].astype(f32)
    for k in range(1, C):
        both = both + w_recv[k].astype(f32)
    wr_recv[my_row] = both.astype(bf16)
    fifth = []
    for m in order:
        copy = remote(
            wr_recv.at[my_row], wr_recv.at[my_row], s5.at[m - 1], r5.at[m - 1], {"row": row_of(m)}
        )
        copy.start()
        fifth.append(copy)
    for copy in fifth:
        copy.wait_recv()
    both = wr_recv[0].astype(f32)
    for m in range(1, R):
        both = both + wr_recv[m].astype(f32)
    gb_ref[...] = both[q : q + 1]
    wc_recv[my_col] = both[0:q].astype(bf16)
    sixth = []
    for k in corder:
        copy = remote(
            wc_recv.at[my_col], wc_recv.at[my_col], s6.at[k - 1], r6.at[k - 1], {"col": col_of(k)}
        )
        copy.start()
        sixth.append(copy)
    for copy in sixth:
        copy.wait_recv()
    for k in range(C):
        gw_ref[pl.ds(k * q, q), :] = wc_recv[k].astype(f32)
    for copy in fourth + fifth + sixth:
        copy.wait_send()
    for k in range(1, C):
        back_copy(k).wait_send()
    for h in range(S):
        for k in range(3):
            sum_to_pair(k, h).wait_send()
        grad_to_pair(place, h, s2.at[0, h]).wait_send()

        @pl.when(inner)
        def _():
            grad_to_inner(place, h, s2b.at[0, h]).wait_send()
            grad_to_inner(0, h, s2b.at[1, h]).wait_send()
            grad_to_pair(2, h, s2.at[1, h]).wait_send()
            grad_to_pair(3, h, s2.at[2, h]).wait_send()


def dense_body(features, weight, bias, tiles, tile_out, tile_in, tile_count, cotangent):
    slots, size = tiles.shape[2], tiles.shape[3]
    n, d = features.shape
    R, C = lax.axis_size("row"), lax.axis_size("col")
    own = n // size
    side, wide = own * R, own * C
    projected = jnp.dot(features, weight, preferred_element_type=jnp.float32).astype(jnp.bfloat16)
    dense = build_dense(
        tiles.reshape(slots, size, size), tile_out.reshape(slots), tile_in.reshape(slots),
        tile_count.reshape(1), side, wide,
    )
    me = lax.axis_index("col")
    inputs = jnp.zeros((wide * size, d), jnp.bfloat16)
    inputs = lax.dynamic_update_slice(inputs, projected, (me * n, 0))
    for m in range(1, C):
        got = lax.ppermute(projected, "col", [(c, (c + m) % C) for c in range(C)])
        inputs = lax.dynamic_update_slice(inputs, got, ((me + C - m) % C * n, 0))
    S = 4
    hb = n // S
    q = d // C
    bf16, f32 = jnp.bfloat16, jnp.float32
    vm = pl.BlockSpec(memory_space=pltpu.VMEM)
    dma = pltpu.SemaphoreType.DMA
    output, gfeat, gw, gb = pl.pallas_call(
        functools.partial(layer_kernel, R, C, S, 1.0 / math.sqrt(n * R * C)),
        out_shape=(
            jax.ShapeDtypeStruct((n, d), bf16),
            jax.ShapeDtypeStruct((n, d), bf16),
            jax.ShapeDtypeStruct((d, d), f32),
            jax.ShapeDtypeStruct((1, d), f32),
        ),
        in_specs=[pl.BlockSpec(memory_space=pl.ANY)] + [vm] * 5,
        out_specs=(vm,) * 4,
        scratch_shapes=[
            pltpu.VMEM((R * n, C * n), bf16),
            pltpu.VMEM((R, S, hb, d), f32),
            pltpu.VMEM((3, S, hb, d), bf16),
            pltpu.VMEM((5, S, hb, d), bf16),
            pltpu.VMEM((hb, d), f32),
            pltpu.VMEM((R, S, d, hb), bf16),
            pltpu.VMEM((C, d, n), f32),
            pltpu.VMEM((C, d, n), bf16),
            pltpu.VMEM((C, d, n), bf16),
            pltpu.VMEM((d, n), f32),
            pltpu.VMEM((C, q + 16, d), bf16),
            pltpu.VMEM((C, q + 16, d), bf16),
            pltpu.VMEM((R, q + 16, d), bf16),
            pltpu.VMEM((C, q, d), bf16),
            dma((R,)), dma((3, S)), dma((5, S)), dma((3, S)), dma((2, S)), dma((R, S)),
            dma((C,)), dma((C,)), dma((C - 1,)), dma((C - 1,)),
            dma((R - 1,)), dma((R - 1,)), dma((C - 1,)), dma((C - 1,)),
        ],
        compiler_params=pltpu.CompilerParams(
            collective_id=0, has_side_effects=True, vmem_limit_bytes=58 * 2**20
        ),
        cost_estimate=pl.CostEstimate(
            flops=4 * n * R * n * C * d, bytes_accessed=2 * n * R * n * C, transcendentals=n * d
        ),
        name="layer",
    )(dense, inputs, features, weight, bias.reshape(1, d), cotangent)
    return output, gfeat, gw, gb.reshape(d)


def layer_body(features, *rest):
    small = lax.axis_size("row") == 4 and lax.axis_size("col") == 4 and features.shape[0] == 512
    return (dense_body if small else body)(features, *rest)


def solution(mesh):
    placed = (
        P(("parts", "row", "col"), None),
        P(),
        P(),
        P(("parts", "row"), "col", None, None, None),
        P(("parts", "row"), "col", None),
        P(("parts", "row"), "col", None),
        P(("parts", "row"), "col"),
        P(("parts", "row", "col"), None),
    )
    return jax.shard_map(
        layer_body,
        mesh=mesh,
        in_specs=placed,
        out_specs=(
            P(("parts", "row", "col"), None),
            P(("parts", "row", "col"), None),
            P("parts", None),
            P("parts"),
        ),
        check_vma=False,
    )
```

```python
import functools
import math

import jax
import jax.numpy as jnp
from jax import lax
from jax.experimental import pallas as pl
from jax.experimental.pallas import tpu as pltpu
from jax.sharding import PartitionSpec as P

MESH = pl.DeviceIdType.MESH


def accumulate(cell_tiles, from_ids, into_ids, live_count, source, into_count, pattern):
    slot_count = cell_tiles.shape[0]
    from_count = source.shape[0]
    cluster_size = source.shape[1]
    feat_width = source.shape[2]
    span_size = 32
    flat_source = source.reshape(from_count, cluster_size * feat_width)
    initial = jnp.zeros((into_count, cluster_size * feat_width), jnp.float32)
    from_range = jnp.arange(from_count, dtype=jnp.int32)
    into_range = jnp.arange(into_count, dtype=jnp.int32)

    def one_block(block_index, running):
        offset = block_index * span_size
        some_tiles = lax.dynamic_slice_in_dim(cell_tiles, offset, span_size, 0)
        from_block = lax.dynamic_slice_in_dim(from_ids, offset, span_size, 0)
        into_block = lax.dynamic_slice_in_dim(into_ids, offset, span_size, 0)
        is_live = offset + jnp.arange(span_size, dtype=jnp.int32) < live_count
        select = (from_block[:, None] == from_range[None, :]).astype(jnp.bfloat16)
        picked = jnp.dot(select, flat_source, preferred_element_type=jnp.float32).astype(
            jnp.bfloat16
        )
        picked = picked.reshape(span_size, cluster_size, feat_width)
        products = jnp.einsum(pattern, some_tiles, picked, preferred_element_type=jnp.float32)
        placing = ((into_range[:, None] == into_block[None, :]) & is_live[None, :]).astype(
            jnp.float32
        )
        added = jnp.dot(
            placing,
            products.reshape(span_size, cluster_size * feat_width),
            precision=lax.Precision.HIGHEST,
            preferred_element_type=jnp.float32,
        )
        return running + added

    block_total = (live_count + span_size - 1) // span_size
    result = lax.fori_loop(0, block_total, one_block, initial)
    return result.reshape(into_count, cluster_size, feat_width)


def slope(hidden, cotangent):
    gate_value = jax.nn.sigmoid(hidden)
    return (
        cotangent.astype(jnp.float32) * gate_value * (1.0 + hidden * (1.0 - gate_value))
    ).astype(jnp.bfloat16)


def body(features, weight, bias, tiles, tile_out, tile_in, tile_count, cotangent):
    slot_count = tiles.shape[2]
    cluster_size = tiles.shape[3]
    feat_width = features.shape[1]
    own_rows = features.shape[0]
    own_clusters = own_rows // cluster_size
    cell_tiles = tiles.reshape(slot_count, cluster_size, cluster_size)
    out_local = tile_out.reshape(slot_count)
    in_local = tile_in.reshape(slot_count)
    live_count = tile_count.reshape(())
    row_devices = lax.axis_size("row")
    col_devices = lax.axis_size("col")
    into_clusters = own_clusters * row_devices
    from_clusters = own_clusters * col_devices
    projected = jnp.dot(features, weight, preferred_element_type=jnp.float32).astype(jnp.bfloat16)
    inputs = lax.all_gather(projected, "col", axis=0, tiled=True)
    partials = accumulate(
        cell_tiles,
        in_local,
        out_local,
        live_count,
        inputs.reshape(from_clusters, cluster_size, feat_width),
        into_clusters,
        "tij,tjd->tid",
    )
    partials = partials.reshape(into_clusters * cluster_size, feat_width)
    summed = lax.psum_scatter(partials, "row", scatter_dimension=0, tiled=True)
    hidden = summed + bias
    output = jax.nn.silu(hidden).astype(jnp.bfloat16)
    own_grad = slope(hidden, cotangent)
    targets = lax.all_gather(own_grad, "row", axis=0, tiled=True)
    grad_partials = accumulate(
        cell_tiles,
        out_local,
        in_local,
        live_count,
        targets.reshape(into_clusters, cluster_size, feat_width),
        from_clusters,
        "tji,tjd->tid",
    )
    grad_partials = grad_partials.reshape(from_clusters * cluster_size, feat_width)
    grad_proj = lax.psum_scatter(grad_partials, "col", scatter_dimension=0, tiled=True).astype(
        jnp.bfloat16
    )
    grad_features = jnp.dot(grad_proj, weight.T, preferred_element_type=jnp.float32).astype(
        jnp.bfloat16
    )
    local_weight = jnp.dot(features.T, grad_proj, preferred_element_type=jnp.float32)
    local_bias = jnp.sum(own_grad.astype(jnp.float32), axis=0)
    grad_weight, grad_bias = lax.psum((local_weight, local_bias), ("row", "col"))
    factor = 1.0 / math.sqrt(own_rows * row_devices * col_devices)
    return (output, grad_features, grad_weight * factor, grad_bias * factor)

def build_kernel(count_ref, out_ids, in_ids, tiles_hbm, dense_hbm, sums, held, dense, in_sem, out_sem):
    slots, size = held.shape[0], held.shape[1]
    side = dense.shape[0] // size
    wide = dense.shape[1] // size
    spare = side * wide
    spans = in_sem.shape[0]
    span = slots // spans

    def fetch(step):
        part = pl.ds(step * span, span)
        return pltpu.make_async_copy(tiles_hbm.at[part], held.at[part], in_sem.at[step])

    for step in range(spans):
        fetch(step).start()

    def clear(at, _):
        sums[at] = jnp.zeros_like(sums[0])
        return 0

    lax.fori_loop(0, spare, clear, 0, unroll=8)

    def add(where, _):
        pair = out_ids[where] * wide + in_ids[where]
        pair = jnp.where(where < count_ref[0], pair, spare)
        sums[pair] += held[where].astype(jnp.float32)
        return 0

    for step in range(spans):
        fetch(step).wait()
        lax.fori_loop(step * span, (step + 1) * span, add, 0, unroll=8)

    def put(o):
        rows = pl.ds(pl.multiple_of(o * size, size), size)
        return pltpu.make_async_copy(dense.at[rows], dense_hbm.at[rows], out_sem.at[o])

    def write(o, _):
        rows = pl.ds(pl.multiple_of(o * size, size), size)
        for i in range(wide):
            dense[rows, pl.ds(i * size, size)] = sums[o * wide + i].astype(jnp.bfloat16)
        put(o).start()
        return 0

    lax.fori_loop(0, side, write, 0)
    for o in range(side):
        put(o).wait()


def build_dense(cell_tiles, out_local, in_local, live_count, side, wide):
    slot_count, size, _ = cell_tiles.shape
    spans = 8
    return pl.pallas_call(
        build_kernel,
        out_shape=jax.ShapeDtypeStruct((side * size, wide * size), jnp.bfloat16),
        grid_spec=pltpu.PrefetchScalarGridSpec(
            num_scalar_prefetch=3,
            grid=(1,),
            in_specs=[pl.BlockSpec(memory_space=pl.ANY)],
            out_specs=pl.BlockSpec(memory_space=pl.ANY),
            scratch_shapes=[
                pltpu.VMEM((side * wide + 1, size, size), jnp.float32),
                pltpu.VMEM((slot_count, size, size), jnp.bfloat16),
                pltpu.VMEM((side * size, wide * size), jnp.bfloat16),
                pltpu.SemaphoreType.DMA((spans,)),
                pltpu.SemaphoreType.DMA((side,)),
            ],
        ),
        compiler_params=pltpu.CompilerParams(vmem_limit_bytes=56 * 2**20),
        cost_estimate=pl.CostEstimate(
            flops=slot_count * size * size * 40, bytes_accessed=4 * slot_count * size * size, transcendentals=0
        ),
        name="dense_cell",
    )(live_count, out_local, in_local, cell_tiles)


def layer_kernel(
    R, C, S, factor,
    a_hbm, p_ref, feat_ref, w_ref, bias_ref, cot_ref,
    out_ref, gfeat_ref, gw_ref, gb_ref,
    a_ref, part, part_send, part_recv, hid, grads, gsum, back_send, back_recv, back_own,
    w_send, w_recv, wr_recv, wc_recv,
    a_sem, s1, r1, s2, s2b, r2, s3, r3, s4, r4, s5, r5, s6, r6,
):
    my_row = lax.axis_index("row")
    my_col = lax.axis_index("col")
    n, d = feat_ref.shape
    hb = n // S
    f32, bf16 = jnp.float32, jnp.bfloat16
    barrier = pltpu.get_barrier_semaphore()

    def row_of(m):
        return lax.rem(my_row + m, R)

    def col_of(m):
        return lax.rem(my_col + m, C)

    for m in range(1, R):
        pl.semaphore_signal(barrier, inc=1, device_id={"row": row_of(m)}, device_id_type=MESH)
    for m in range(1, C):
        pl.semaphore_signal(barrier, inc=1, device_id={"col": col_of(m)}, device_id_type=MESH)

    def remote(src, dst, send, recv, where):
        return pltpu.make_async_remote_copy(
            src_ref=src, dst_ref=dst, send_sem=send, recv_sem=recv, device_id=where, device_id_type=MESH
        )

    order = [2, 1, 3]
    corder = [2, 3, 1]

    high = my_row // 2
    place = (1 - high) * my_row + high * (R - 1 - my_row)

    def at(p):
        return (1 - high) * p + high * (R - 1 - p)

    pair_row = at(1 - place)
    next_row = at(place + 1)
    inner_row = at(2)
    outer, inner = place == 0, place == 1

    targets = [at(3), at(2), pair_row, my_row]
    fetches = []
    for k in range(R):
        rows = pl.ds(pl.multiple_of(targets[k] * n, n), n)
        fetches.append(pltpu.make_async_copy(a_hbm.at[rows], a_ref.at[rows], a_sem.at[k]))
        fetches[k].start()

    def sum_to_pair(k, h):
        return remote(
            part_send.at[k, h], part_recv.at[k, h], s1.at[k, h], r1.at[k, h], {"row": pair_row}
        )

    def sum_to_inner(k, h):
        return remote(
            part_send.at[k, h], part_recv.at[k + 3, h], s1.at[k, h], r1.at[k + 3, h], {"row": inner_row}
        )

    pl.semaphore_wait(barrier, R + C - 2)
    for h in range(S):
        for k in range(R):
            if h == 0:
                fetches[k].wait()
            start = pl.multiple_of(targets[k] * n + h * hb, hb)
            part[k, h] = jnp.dot(a_ref[pl.ds(start, hb), :], p_ref[...], preferred_element_type=f32)
            if k < 3:

                @pl.when(outer)
                def _():
                    part_send[k, h] = part[k, h].astype(bf16)
                    sum_to_pair(k, h).start()

    def grad_to_pair(p, h, sem):
        row = at(p)
        return remote(grads.at[row, h], grads.at[row, h], sem, r2.at[row, h], {"row": pair_row})

    def grad_to_inner(p, h, sem):
        row = at(p)
        return remote(grads.at[row, h], grads.at[row, h], sem, r2.at[row, h], {"row": inner_row})

    gbias = jnp.zeros((1, d), f32)
    own_cols = [3, 2, 1, 0]

    def col_block(k):
        chip, core = my_col // 2, lax.rem(my_col, 2)
        chip = 1 - chip if k >= 2 else chip
        core = 1 - core if k % 2 else core
        return chip * 2 + core

    def back(p, h, first, last):
        row = at(p)
        start = pl.multiple_of(row * n + h * hb, hb)
        for k in own_cols:
            c0 = pl.multiple_of(col_block(k) * n, n)
            new = jnp.dot(
                grads[row, h], a_ref[pl.ds(start, hb), pl.ds(c0, n)], preferred_element_type=f32
            )
            if not first:
                new = gsum[k] + new
            gsum[k] = new
            if last and k in (3, 1):
                back_send[k] = new.astype(bf16)
                back_copy(k).start()

    def back_copy(k):
        if k == 2:
            return remote(back_send.at[2], back_recv.at[2], s3.at[2], r3.at[2], {"col": col_block(2)})
        return remote(back_send.at[k], back_recv.at[k], s3.at[k], r3.at[k], {"col": col_block(1)})

    for h in range(S + 1):
        if h < S:

            @pl.when(inner)
            def _():
                for k in range(3):
                    if k < 2:
                        sum_to_pair(k, h).wait_recv()
                        got = part_recv[k, h]
                    else:
                        sum_to_inner(0, h).wait_recv()
                        got = part_recv[3, h]
                    part_send[k, h] = (part[k, h] + got.astype(f32)).astype(bf16)
                    if k < 2:
                        sum_to_inner(k, h).start()
                    else:
                        sum_to_pair(k, h).start()

            rows = pl.ds(h * hb, hb)
            sum_to_pair(2, h).wait_recv()
            hid[...] = part[3, h] + bias_ref[...] + part_recv[2, h].astype(f32)

            @pl.when(inner)
            def _():
                sum_to_inner(1, h).wait_recv()
                hid[...] += part_recv[4, h].astype(f32)

            hidden = hid[...]
            gate = jax.nn.sigmoid(hidden)
            g = cot_ref[rows, :].astype(f32) * gate * (1.0 + hidden * (1.0 - gate))
            g = g.astype(bf16).astype(f32)
            grads[my_row, h] = g.T.astype(bf16)
            grad_to_pair(place, h, s2.at[0, h]).start()

            @pl.when(inner)
            def _():
                grad_to_inner(place, h, s2b.at[0, h]).start()

            out_ref[rows, :] = (hidden * gate).astype(bf16)
            gbias = gbias + jnp.sum(g, axis=0, keepdims=True)
        if h > 0:
            e = h - 1
            back(place, e, e == 0, False)
            for j, p in enumerate([1 - place, 2, 3]):
                grad_to_pair(p, e, s2.at[0, e]).wait_recv()

                @pl.when(inner)
                def _():
                    if j == 0:
                        grad_to_inner(p, e, s2b.at[1, e]).start()
                    else:
                        grad_to_pair(p, e, s2.at[j, e]).start()

                back(p, e, False, e == S - 1 and j == 2)

    back_copy(3).wait_recv()
    back_send[2] = (gsum[2] + back_recv[3].astype(f32)).astype(bf16)
    back_copy(2).start()
    back_copy(1).wait_recv()
    total = gsum[0] + back_recv[1].astype(f32)
    back_copy(2).wait_recv()
    total = total + back_recv[2].astype(f32)
    gproj = total.astype(bf16)
    gweight = jnp.dot(gproj, feat_ref[...], preferred_element_type=f32).T * factor
    gbias = gbias * factor
    q = d // C
    for k in range(C):
        w_send[k, 0:q] = gweight[k * q : (k + 1) * q].astype(bf16)
        w_send[k, q : q + 16] = jnp.broadcast_to(gbias, (16, d)).astype(bf16)
    fourth = []
    for k in corder:
        copy = remote(
            w_send.at[col_of(k)], w_recv.at[my_col], s4.at[k - 1], r4.at[k - 1], {"col": col_of(k)}
        )
        copy.start()
        fourth.append(copy)
    w_recv[my_col] = w_send[my_col]
    back_own[...] = jnp.dot(w_ref[...], gproj, preferred_element_type=f32)
    gfeat_ref[...] = back_own[...].T.astype(bf16)
    for copy in fourth:
        copy.wait_recv()
    both = w_recv[0].astype(f32)
    for k in range(1, C):
        both = both + w_recv[k].astype(f32)
    wr_recv[my_row] = both.astype(bf16)
    fifth = []
    for m in order:
        copy = remote(
            wr_recv.at[my_row], wr_recv.at[my_row], s5.at[m - 1], r5.at[m - 1], {"row": row_of(m)}
        )
        copy.start()
        fifth.append(copy)
    for copy in fifth:
        copy.wait_recv()
    both = wr_recv[0].astype(f32)
    for m in range(1, R):
        both = both + wr_recv[m].astype(f32)
    gb_ref[...] = both[q : q + 1]
    wc_recv[my_col] = both[0:q].astype(bf16)
    sixth = []
    for k in corder:
        copy = remote(
            wc_recv.at[my_col], wc_recv.at[my_col], s6.at[k - 1], r6.at[k - 1], {"col": col_of(k)}
        )
        copy.start()
        sixth.append(copy)
    for copy in sixth:
        copy.wait_recv()
    for k in range(C):
        gw_ref[pl.ds(k * q, q), :] = wc_recv[k].astype(f32)
    for copy in fourth + fifth + sixth:
        copy.wait_send()
    for k in range(1, C):
        back_copy(k).wait_send()
    for h in range(S):
        for k in range(3):
            sum_to_pair(k, h).wait_send()
        grad_to_pair(place, h, s2.at[0, h]).wait_send()

        @pl.when(inner)
        def _():
            grad_to_inner(place, h, s2b.at[0, h]).wait_send()
            grad_to_inner(0, h, s2b.at[1, h]).wait_send()
            grad_to_pair(2, h, s2.at[1, h]).wait_send()
            grad_to_pair(3, h, s2.at[2, h]).wait_send()


def dense_body(features, weight, bias, tiles, tile_out, tile_in, tile_count, cotangent):
    slots, size = tiles.shape[2], tiles.shape[3]
    n, d = features.shape
    R, C = lax.axis_size("row"), lax.axis_size("col")
    own = n // size
    side, wide = own * R, own * C
    projected = jnp.dot(features, weight, preferred_element_type=jnp.float32).astype(jnp.bfloat16)
    dense = build_dense(
        tiles.reshape(slots, size, size), tile_out.reshape(slots), tile_in.reshape(slots),
        tile_count.reshape(1), side, wide,
    )
    me = lax.axis_index("col")
    inputs = jnp.zeros((wide * size, d), jnp.bfloat16)
    inputs = lax.dynamic_update_slice(inputs, projected, (me * n, 0))
    for m in range(1, C):
        got = lax.ppermute(projected, "col", [(c, (c + m) % C) for c in range(C)])
        inputs = lax.dynamic_update_slice(inputs, got, ((me + C - m) % C * n, 0))
    S = 2
    hb = n // S
    q = d // C
    bf16, f32 = jnp.bfloat16, jnp.float32
    vm = pl.BlockSpec(memory_space=pltpu.VMEM)
    dma = pltpu.SemaphoreType.DMA
    output, gfeat, gw, gb = pl.pallas_call(
        functools.partial(layer_kernel, R, C, S, 1.0 / math.sqrt(n * R * C)),
        out_shape=(
            jax.ShapeDtypeStruct((n, d), bf16),
            jax.ShapeDtypeStruct((n, d), bf16),
            jax.ShapeDtypeStruct((d, d), f32),
            jax.ShapeDtypeStruct((1, d), f32),
        ),
        in_specs=[pl.BlockSpec(memory_space=pl.ANY)] + [vm] * 5,
        out_specs=(vm,) * 4,
        scratch_shapes=[
            pltpu.VMEM((R * n, C * n), bf16),
            pltpu.VMEM((R, S, hb, d), f32),
            pltpu.VMEM((3, S, hb, d), bf16),
            pltpu.VMEM((5, S, hb, d), bf16),
            pltpu.VMEM((hb, d), f32),
            pltpu.VMEM((R, S, d, hb), bf16),
            pltpu.VMEM((C, d, n), f32),
            pltpu.VMEM((C, d, n), bf16),
            pltpu.VMEM((C, d, n), bf16),
            pltpu.VMEM((d, n), f32),
            pltpu.VMEM((C, q + 16, d), bf16),
            pltpu.VMEM((C, q + 16, d), bf16),
            pltpu.VMEM((R, q + 16, d), bf16),
            pltpu.VMEM((C, q, d), bf16),
            dma((R,)), dma((3, S)), dma((5, S)), dma((3, S)), dma((2, S)), dma((R, S)),
            dma((C,)), dma((C,)), dma((C - 1,)), dma((C - 1,)),
            dma((R - 1,)), dma((R - 1,)), dma((C - 1,)), dma((C - 1,)),
        ],
        compiler_params=pltpu.CompilerParams(
            collective_id=0, has_side_effects=True, vmem_limit_bytes=48 * 2**20
        ),
        cost_estimate=pl.CostEstimate(
            flops=4 * n * R * n * C * d, bytes_accessed=2 * n * R * n * C, transcendentals=n * d
        ),
        name="layer",
    )(dense, inputs, features, weight, bias.reshape(1, d), cotangent)
    return output, gfeat, gw, gb.reshape(d)


def layer_body(features, *rest):
    small = lax.axis_size("row") == 4 and lax.axis_size("col") == 4 and features.shape[0] == 512
    return (dense_body if small else body)(features, *rest)


def solution(mesh):
    placed = (
        P(("parts", "row", "col"), None),
        P(),
        P(),
        P(("parts", "row"), "col", None, None, None),
        P(("parts", "row"), "col", None),
        P(("parts", "row"), "col", None),
        P(("parts", "row"), "col"),
        P(("parts", "row", "col"), None),
    )
    return jax.shard_map(
        layer_body,
        mesh=mesh,
        in_specs=placed,
        out_specs=(
            P(("parts", "row", "col"), None),
            P(("parts", "row", "col"), None),
            P("parts", None),
            P("parts"),
        ),
        check_vma=False,
    )
```
